32 devices in a mesh: group: 2 (over core), dp: 2 (over x), mp: 8 (over z, y).
Axes of the slice: x: 2, y: 2, z: 4, core: 2. Of those that a mesh axis runs over, the one named last changes fastest.
Arguments:
- latents: float32 [4, 320, 2432], P(('group', 'dp')), may hold values from -6 to 6
- noise: bfloat16 [4, 2, 320, 2432], P(('group', 'dp')), may hold values from -6 to 6
- ref_velocity: bfloat16 [4, 2, 320, 2432], P(('group', 'dp')), may hold values from -6 to 6
- start_step: int32 [4], P(('group', 'dp')), may hold values from 1 to 6
- advantages: float32 [4], P(('group', 'dp')), may hold values from -4 to 4
- behaviour_gap: float32 [4, 2], P(('group', 'dp')), may hold values from -0.4 to 0.4
- modulation: float32 [10, 2, 2432], replicated, may hold values from -3 to 3
- w_in: bfloat16 [2432, 9728], P(('group', 'dp'), 'mp'), may hold values from -6 to 6
- w_down: bfloat16 [2432, 9728], P(('group', 'dp'), 'mp'), may hold values from -6 to 6
Outputs:
- final_latents: float32 [4, 320, 2432], P(('group', 'dp'))
- new_w_in: bfloat16 [2432, 9728], P(('group', 'dp'), 'mp')
- new_w_down: bfloat16 [2432, 9728], P(('group', 'dp'), 'mp')
The draws below stay inside these ranges and needn't reach their ends.
Inputs may be any that keep to these rules, and one draw needn't show every extreme that they name: `start_step`: the second step of an image is at the next plan position.
All inputs are finite; a program needn't handle non-finite values.
Results may differ from the reference program's by a relative error of at most 0.014.
Values may be sent and summed in bfloat16 or wider, within the bound.
A program may use at most 128 MiB of HBM per device.

```python
import math
import jax
import jax.numpy as jnp
from jax import lax

D = 2432
FF = 9728
LEN = 320
SCHED = 10
IMAGES = 4


def set_ends(array, rng, least, largest):
    index_at = [jax.random.randint(jax.random.fold_in(rng, axis), (), 0, length) for axis, length in enumerate(array.shape)]
    main_axis = array.shape.index(max(array.shape))
    neighbour = index_at[:main_axis] + [(index_at[main_axis] + 1) % array.shape[main_axis]] + index_at[main_axis + 1:]
    return array.at[tuple(index_at)].set(least).at[tuple(neighbour)].set(largest)


def block_levels(key, shape, cuts, low, largest):
    factor_of, own = 1.0, jax.random.fold_in(key, 6)
    for axis_at, parts in cuts:
        heights = jnp.exp(jax.random.uniform(jax.random.fold_in(own, axis_at), (parts,), jnp.float32, low / len(cuts), largest / len(cuts)))
        factor_of = factor_of * jnp.repeat(heights, shape[axis_at] // parts).reshape([-1 if axis == axis_at else 1 for axis in range(len(shape))])
    return factor_of


def centred(key, extent, spread, reach, split=(), held_as=jnp.bfloat16):
    factor_of = block_levels(key, extent, split, -0.22, 0.18) if split else 1.0
    result = jax.random.normal(key, extent, jnp.float32) * spread * factor_of
    return jnp.minimum(jnp.maximum(result, -reach), reach).astype(held_as)


def setup_inputs(seed: int = 0) -> dict:
    seeds = jax.random.split(jax.random.key(seed), 10)
    latents = centred(seeds[0], (IMAGES, LEN, D), 1.0, 6.0, ((0, 4),), jnp.float32)
    noise = centred(seeds[1], (IMAGES, 2, LEN, D), 1.0, 6.0, ((0, 4),))
    ref_velocity = centred(seeds[2], (IMAGES, 2, LEN, D), 1.0, 6.0, ((0, 4),))
    start_step = set_ends(jax.random.randint(seeds[3], (IMAGES,), 1, 7), jax.random.fold_in(seeds[3], 1), 1, 6).astype(jnp.int32)
    advantages = centred(seeds[4], (IMAGES,), 1.0, 4.0, ((0, 4),), jnp.float32)
    behaviour_gap = jnp.clip(jax.random.uniform(seeds[5], (IMAGES, 2), jnp.float32, -0.4, 0.4) * block_levels(seeds[5], (IMAGES, 2), ((0, 4),), -0.4, 0.0), -0.4, 0.4)
    modulation = centred(seeds[6], (SCHED, 2, D), 0.5, 3.0, (), jnp.float32)
    w_in = centred(seeds[7], (D, FF), 1.0, 6.0, ((0, 4), (1, 8)))
    w_down = centred(seeds[8], (D, FF), 1.0, 6.0, ((0, 4), (1, 8)))
    return {"latents": latents, "noise": noise, "ref_velocity": ref_velocity, "start_step": start_step, "advantages": advantages, "behaviour_gap": behaviour_gap, "modulation": modulation, "w_in": w_in, "w_down": w_down}


NOISE_SLOPE = 0.7
CLIP_RANGE = 0.2
GELU_COEF = 0.7978845608028654
GELU_CUBE = 0.044715
HIGH_PREC = lax.Precision.HIGHEST

def gelu_parts(pre_act):
    tangent = jnp.tanh(GELU_COEF * (pre_act + GELU_CUBE * pre_act * pre_act * pre_act))
    activation = 0.5 * pre_act * (1.0 + tangent)
    gelu_slope = 0.5 * (1.0 + tangent) + 0.5 * pre_act * (1.0 - tangent * tangent) * GELU_COEF * (1.0 + 3.0 * GELU_CUBE * pre_act * pre_act)
    return (activation, gelu_slope)

def reference(latents, noise, ref_velocity, start_step, advantages, behaviour_gap, modulation, w_in, w_down):
    model_width = latents.shape[2]
    hidden_width = w_in.shape[1]
    step_len = 1.0 / SCHED
    vel_coef = 1.0 + 0.5 * NOISE_SLOPE * NOISE_SLOPE
    latent_now = jnp.transpose(latents, (1, 0, 2))
    w_in_wide = w_in.astype(jnp.float32)
    w_down_wide = w_down.astype(jnp.float32)
    grad_in = jnp.zeros((model_width, hidden_width), jnp.float32)
    grad_down = jnp.zeros((model_width, hidden_width), jnp.float32)
    for step_num in range(2):
        sched_index = start_step + step_num
        time_now = 1.0 - sched_index.astype(jnp.float32) / SCHED
        onehot = (sched_index[:, None] == jnp.arange(SCHED, dtype=jnp.int32)[None, :]).astype(jnp.float32)
        mod_rows = jnp.einsum('is,scd->icd', onehot, modulation, precision=HIGH_PREC)
        normed = latent_now * lax.rsqrt(lax.optimization_barrier(jnp.mean(latent_now * latent_now, axis=2, keepdims=True)) + 1e-06)
        inputs = (normed * (1.0 + mod_rows[None, :, 1, :]) + mod_rows[None, :, 0, :]).astype(jnp.bfloat16)
        pre_act = jnp.einsum('lid,df->lif', inputs.astype(jnp.float32), w_in_wide, precision=HIGH_PREC) / math.sqrt(model_width)
        activation, gelu_slope = gelu_parts(pre_act)
        hidden = activation.astype(jnp.bfloat16)
        velocity = jnp.einsum('lif,df->lid', hidden.astype(jnp.float32), w_down_wide, precision=HIGH_PREC) / math.sqrt(hidden_width)
        noise_level = (NOISE_SLOPE * jnp.sqrt(time_now / (1.0 - time_now)))[None, :, None]
        drift_x = (0.5 * NOISE_SLOPE * NOISE_SLOPE / (1.0 - time_now))[None, :, None]
        eps_draw = jnp.transpose(noise[:, step_num], (1, 0, 2)).astype(jnp.float32)
        ref_vel = jnp.transpose(ref_velocity[:, step_num], (1, 0, 2)).astype(jnp.float32)
        step_mean = latent_now * (1.0 - step_len * drift_x) - step_len * vel_coef * velocity
        latent_next = step_mean + noise_level * math.sqrt(step_len) * eps_draw
        policy_ratio = jnp.exp(behaviour_gap[:, step_num])
        active = (advantages >= 0.0) & (policy_ratio <= 1.0 + CLIP_RANGE) | (advantages < 0.0) & (policy_ratio >= 1.0 - CLIP_RANGE)
        pg_coef = jnp.where(active, policy_ratio * advantages, jnp.zeros_like(advantages))[None, :, None]
        vel_grad = (pg_coef * vel_coef * math.sqrt(step_len) * eps_draw / noise_level + vel_coef * vel_coef * step_len * (velocity - ref_vel) / (noise_level * noise_level)).astype(jnp.bfloat16)
        hid_grad = jnp.einsum('lid,df->lif', vel_grad.astype(jnp.float32), w_down_wide, precision=HIGH_PREC) / math.sqrt(hidden_width)
        pre_grad = (hid_grad * gelu_slope).astype(jnp.bfloat16)
        grad_in = grad_in + jnp.einsum('lid,lif->df', inputs.astype(jnp.float32), pre_grad.astype(jnp.float32), precision=HIGH_PREC) / math.sqrt(model_width)
        grad_down = grad_down + jnp.einsum('lid,lif->df', vel_grad.astype(jnp.float32), hidden.astype(jnp.float32), precision=HIGH_PREC) / math.sqrt(hidden_width)
        latent_now = latent_next
    total = jnp.sum(grad_in * grad_in) + jnp.sum(grad_down * grad_down)
    grad_rms = jnp.sqrt(total / (2.0 * model_width * hidden_width) + 1e-06)
    new_w_in = (w_in_wide - grad_in / grad_rms).astype(jnp.bfloat16)
    new_w_down = (w_down_wide - grad_down / grad_rms).astype(jnp.bfloat16)
    return (jnp.transpose(latent_now, (1, 0, 2)), new_w_in, new_w_down)
```

```python
import functools
import math

import jax
import jax.numpy as jnp
from jax import lax
from jax.experimental import pallas as pl
from jax.experimental.pallas import tpu as pltpu
from jax.sharding import PartitionSpec as P

SCHED = 10


NOISE_SLOPE = 0.7
CLIP_RANGE = 0.2
GELU_COEF = 0.7978845608028654
GELU_CUBE = 0.044715
HIGH_PREC = lax.Precision.HIGHEST
MESH = pl.DeviceIdType.MESH
F32 = jnp.float32
BF16 = jnp.bfloat16
VMEM_LIMIT = 56 * 1024 * 1024


def params(collective_id):
    return pltpu.CompilerParams(
        collective_id=collective_id, has_side_effects=True, vmem_limit_bytes=VMEM_LIMIT
    )


def remote(src, dst, send_sem, recv_sem, **axes):
    return pltpu.make_async_remote_copy(
        src_ref=src, dst_ref=dst, send_sem=send_sem, recv_sem=recv_sem,
        device_id=axes, device_id_type=MESH,
    )


def greet(peers):
    barrier = pltpu.get_barrier_semaphore()
    for axes in peers:
        pl.semaphore_signal(barrier, inc=1, device_id=axes, device_id_type=MESH)
    pl.semaphore_wait(barrier, len(peers))


def row_chunks(rows):
    parts = 2 if rows % 32 == 0 else 1
    size = rows // parts
    return [pl.ds(c * size, size) for c in range(parts)]


def gather_kernel(nd, w_in, w_down, out_in, out_down, xs, xr, fs, fr, os, orr, ls):
    g, d = lax.axis_index("group"), lax.axis_index("dp")
    other = 1 - g
    targets = [lax.rem(d + o, nd) for o in range(nd)]
    sources = [lax.rem(d - o + nd, nd) for o in range(nd)]
    greet([{"group": other}] + [{"dp": targets[o]} for o in range(1, nd)])
    chunks = row_chunks(w_in.shape[0])
    mine = g * nd + d
    pairs = ((w_in, out_in), (w_down, out_down))
    pending = []
    for a, (src, dst) in enumerate(pairs):
        for c, rows in enumerate(chunks):
            for o in range(1, nd):
                copy = remote(src.at[rows], dst.at[mine, rows], xs.at[a, c, o], xr.at[a, c, o], dp=targets[o])
                copy.start()
                pending.append(copy)
    local = []
    for a, (src, dst) in enumerate(pairs):
        copy = remote(src, dst.at[mine], os.at[a], orr.at[a], group=other)
        copy.start()
        pending.append(copy)
        keep = pltpu.make_async_copy(src, dst.at[mine], ls.at[a])
        keep.start()
        local.append(keep)
    for a, (src, dst) in enumerate(pairs):
        for c, rows in enumerate(chunks):
            for o in range(1, nd):
                block = g * nd + sources[o]
                remote(src.at[rows], dst.at[block, rows], xs.at[a, c, o], xr.at[a, c, o], dp=targets[o]).wait_recv()
                copy = remote(dst.at[block, rows], dst.at[block, rows], fs.at[a, c, o], fr.at[a, c, o], group=other)
                copy.start()
                pending.append(copy)
    for a, (src, dst) in enumerate(pairs):
        remote(src, dst.at[other * nd + d], os.at[a], orr.at[a], group=other).wait_recv()
        for c, rows in enumerate(chunks):
            for o in range(1, nd):
                block = other * nd + sources[o]
                remote(dst.at[block, rows], dst.at[block, rows], fs.at[a, c, o], fr.at[a, c, o], group=other).wait_recv()
    for copy in pending:
        copy.wait_send()
    for copy in local:
        copy.wait()


def gather_weights(w_in, w_down, ng, nd):
    rows, units = w_in.shape
    nc = len(row_chunks(rows))
    dma = pltpu.SemaphoreType.DMA
    shape = jax.ShapeDtypeStruct((ng * nd, rows, units), w_in.dtype)
    full_in, full_down = pl.pallas_call(
        functools.partial(gather_kernel, nd),
        out_shape=(shape, shape),
        in_specs=[pl.BlockSpec(memory_space=pl.ANY)] * 2,
        out_specs=(pl.BlockSpec(memory_space=pl.ANY),) * 2,
        scratch_shapes=[
            dma((2, nc, nd)), dma((2, nc, nd)), dma((2, nc, nd)), dma((2, nc, nd)),
            dma((2,)), dma((2,)), dma((2,)),
        ],
        compiler_params=params(1),
        name="gather_weights",
    )(w_in, w_down)
    return full_in.reshape(ng * nd * rows, units), full_down.reshape(ng * nd * rows, units)


def sum_kernel(no, src, out, ybuf, zsum, zbuf, ys, yr, zs, zr, gzs, gzr, gys, gyr):
    m = lax.axis_index("mp")
    y, z = lax.rem(m, 2), lax.div(m, 2)
    partner = z * 2 + 1 - y
    ahead = [lax.rem(z + o, no) for o in range(no)]
    behind = [lax.rem(z - o + no, no) for o in range(no)]
    greet([{"mp": partner}] + [{"mp": ahead[o] * 2 + y} for o in range(1, no)])
    order = list(range(1, no)) + [0]
    pending = []
    for o in order:
        copy = remote(src.at[ahead[o] * 2 + 1 - y], ybuf.at[o], ys.at[o], yr.at[o], mp=partner)
        copy.start()
        pending.append(copy)
    for o in order[:-1]:
        remote(src.at[ahead[o] * 2 + 1 - y], ybuf.at[o], ys.at[o], yr.at[o], mp=partner).wait_recv()
        zsum[o] = (src[ahead[o] * 2 + y].astype(F32) + ybuf[o].astype(F32)).astype(BF16)
        copy = remote(zsum.at[o], zbuf.at[o], zs.at[o], zr.at[o], mp=ahead[o] * 2 + y)
        copy.start()
        pending.append(copy)
    remote(src.at[z * 2 + 1 - y], ybuf.at[0], ys.at[0], yr.at[0], mp=partner).wait_recv()
    total = src[m].astype(F32) + ybuf[0].astype(F32)
    for o in range(1, no):
        remote(zsum.at[o], zbuf.at[o], zs.at[o], zr.at[o], mp=ahead[o] * 2 + y).wait_recv()
        total = total + zbuf[o].astype(F32)
    out[m] = total.astype(BF16)
    for o in range(1, no):
        copy = remote(out.at[m], out.at[m], gzs.at[o], gzr.at[o], mp=ahead[o] * 2 + y)
        copy.start()
        pending.append(copy)
    copy = remote(out.at[m], out.at[m], gys.at[0], gyr.at[0], mp=partner)
    copy.start()
    pending.append(copy)
    for o in range(1, no):
        block = out.at[behind[o] * 2 + y]
        remote(block, block, gzs.at[o], gzr.at[o], mp=ahead[o] * 2 + y).wait_recv()
        copy = remote(block, block, gys.at[o], gyr.at[o], mp=partner)
        copy.start()
        pending.append(copy)
    for o in range(no):
        block = out.at[behind[o] * 2 + 1 - y]
        remote(block, block, gys.at[o], gyr.at[o], mp=partner).wait_recv()
    for copy in pending:
        copy.wait_send()


def sum_over_mp(part, n, collective_id):
    images, tokens, width = part.shape
    no, rows = n // 2, images * tokens // n
    dma = pltpu.SemaphoreType.DMA
    vmem = pl.BlockSpec(memory_space=pltpu.VMEM)
    summed = pl.pallas_call(
        functools.partial(sum_kernel, no),
        out_shape=jax.ShapeDtypeStruct((n, rows, width), BF16),
        in_specs=[vmem],
        out_specs=vmem,
        scratch_shapes=[pltpu.VMEM((no, rows, width), BF16)] * 3 + [dma((no,))] * 8,
        compiler_params=params(collective_id),
        name="sum_over_mp",
    )(part.reshape(n, rows, width))
    return summed.reshape(images, tokens, width)


def update_kernel(
    nd, n, count, g_in, g_down, w_in, w_down, new_in, new_down,
    own, sib, far, total, sq_mp, sq_gd, cs, cr, xs, xr, ls, ms, mr, ps, pr,
):
    g, d, m = lax.axis_index("group"), lax.axis_index("dp"), lax.axis_index("mp")
    other = 1 - g
    targets = [lax.rem(d + o, nd) for o in range(nd)]
    mp_peers = [lax.rem(m + o, n) for o in range(n)]
    gd_peers = [(h, o) for h in range(2) for o in range(nd)]
    place = lambda h: g if h == 0 else other
    greet(
        [{"group": place(h), "dp": targets[o]} for h, o in gd_peers[1:]]
        + [{"mp": mp_peers[o]} for o in range(1, n)]
    )
    rows = w_in.shape[0]
    chunks = row_chunks(rows)
    order = list(range(1, nd)) + [0]
    grads = (g_in, g_down)
    pending = []
    loads = {}
    for o in order:
        for a in range(2):
            for c, part in enumerate(chunks):
                copy = remote(
                    grads[a].at[other * nd + targets[o], part], sib.at[a, o, part],
                    cs.at[a, o, c], cr.at[a, o, c], group=other,
                )
                copy.start()
                pending.append(copy)
                load = pltpu.make_async_copy(
                    grads[a].at[g * nd + targets[o], part], own.at[a, o, part], ls.at[a, o, c]
                )
                load.start()
                loads[a, o, c] = (load, copy)
    step = 16
    def tiles(part, body, init):
        return lax.fori_loop(0, part.size // step, lambda i, v: body(pl.ds(pl.multiple_of(part.start + i * step, step), step), v), init)
    for o in order[:-1]:
        for a in range(2):
            for c, part in enumerate(chunks):
                load, copy = loads[a, o, c]
                load.wait()
                copy.wait_recv()
                def add(at, _):
                    sib[a, o, at] = (sib[a, o, at].astype(F32) + own[a, o, at].astype(F32)).astype(BF16)
                    return 0
                tiles(part, add, 0)
                send = remote(sib.at[a, o, part], far.at[a, o - 1, part], xs.at[a, o, c], xr.at[a, o, c], dp=targets[o])
                send.start()
                pending.append(send)
                loads[a, o, c] = send
    square = jnp.zeros((step, w_in.shape[1]), F32)
    for a in range(2):
        for c, part in enumerate(chunks):
            load, copy = loads[a, 0, c]
            load.wait()
            copy.wait_recv()
            def near(at, _):
                total[a, at] = sib[a, 0, at].astype(F32) + own[a, 0, at].astype(F32)
                return 0
            tiles(part, near, 0)
    for a in range(2):
        for c, part in enumerate(chunks):
            for o in order[:-1]:
                loads[a, o, c].wait_recv()
            def finish(at, sq):
                value = total[a, at]
                for o in order[:-1]:
                    value = value + far[a, o - 1, at].astype(F32)
                total[a, at] = value
                return sq + value * value
            square = tiles(part, finish, square)
    sq_mp[0] = jnp.full((8, 128), jnp.sum(square), F32)
    sends = []
    for o in range(1, n):
        copy = remote(sq_mp.at[0], sq_mp.at[o], ms.at[o], mr.at[o], mp=mp_peers[o])
        copy.start()
        sends.append(copy)
    for copy in sends:
        copy.wait_recv()
    pending += sends
    value = sq_mp[0]
    for o in range(1, n):
        value = value + sq_mp[o]
    sq_gd[0] = value
    sends = []
    for p, (h, o) in enumerate(gd_peers):
        if p:
            copy = remote(sq_gd.at[0], sq_gd.at[p], ps.at[p], pr.at[p], group=place(h), dp=targets[o])
            copy.start()
            sends.append(copy)
    for copy in sends:
        copy.wait_recv()
    pending += sends
    for p in range(1, len(gd_peers)):
        value = value + sq_gd[p]
    inverse = lax.rsqrt(value[0:1, 0:1] / count + 1e-06)
    for a, (w, new) in enumerate(((w_in, new_in), (w_down, new_down))):
        def update(at, _):
            new[at] = (w[at].astype(F32) - total[a, at] * inverse).astype(BF16)
            return 0
        tiles(pl.ds(0, rows), update, 0)
    for copy in pending:
        copy.wait_send()


def update_weights(grad_in, grad_down, w_in, w_down, ng, nd, n):
    rows, units = w_in.shape
    nc = len(row_chunks(rows))
    count = 2.0 * rows * ng * nd * units * n
    dma = pltpu.SemaphoreType.DMA
    vmem = pl.BlockSpec(memory_space=pltpu.VMEM)
    hbm = pl.BlockSpec(memory_space=pl.ANY)
    shape = jax.ShapeDtypeStruct((rows, units), w_in.dtype)
    return pl.pallas_call(
        functools.partial(update_kernel, nd, n, count),
        out_shape=(shape, shape),
        in_specs=[hbm, hbm, vmem, vmem],
        out_specs=(vmem, vmem),
        scratch_shapes=[
            pltpu.VMEM((2, nd, rows, units), BF16),
            pltpu.VMEM((2, nd, rows, units), BF16),
            pltpu.VMEM((2, nd - 1, rows, units), BF16),
            pltpu.VMEM((2, rows, units), F32),
            pltpu.VMEM((n, 8, 128), F32),
            pltpu.VMEM((ng * nd, 8, 128), F32),
            dma((2, nd, nc)), dma((2, nd, nc)), dma((2, nd, nc)), dma((2, nd, nc)), dma((2, nd, nc)),
            dma((n,)), dma((n,)), dma((ng * nd,)), dma((ng * nd,)),
        ],
        compiler_params=params(4),
        name="update_weights",
    )(grad_in.reshape(ng * nd, rows, units), grad_down.reshape(ng * nd, rows, units), w_in, w_down)


def update_by_ops(grad_in, grad_down, w_in, w_down, ng, nd, n):
    rows, units = w_in.shape
    count = 2.0 * rows * ng * nd * units * n
    mine = [
        lax.psum_scatter(grad, ("group", "dp"), scatter_dimension=0, tiled=True).astype(F32)
        for grad in (grad_in, grad_down)
    ]
    total = lax.psum(sum(jnp.sum(grad * grad) for grad in mine), ("group", "dp", "mp"))
    rms = jnp.sqrt(total / count + 1e-06)
    return tuple(
        (w.astype(F32) - grad / rms).astype(BF16) for w, grad in zip((w_in, w_down), mine)
    )


def gelu_parts(pre_act):
    tangent = jnp.tanh(GELU_COEF * (pre_act + GELU_CUBE * pre_act * pre_act * pre_act))
    activation = 0.5 * pre_act * (1.0 + tangent)
    gelu_slope = 0.5 * (1.0 + tangent) + 0.5 * pre_act * (1.0 - tangent * tangent) * GELU_COEF * (
        1.0 + 3.0 * GELU_CUBE * pre_act * pre_act
    )
    return (activation, gelu_slope)


def on_device(
    latents, noise, ref_velocity, start_step, advantages, behaviour_gap, modulation, w_in, w_down
):
    model_width = latents.shape[2]
    shard_units = w_in.shape[1]
    ng, nd, n = lax.axis_size("group"), lax.axis_size("dp"), lax.axis_size("mp")
    hidden_width = shard_units * n
    step_len = 1.0 / SCHED
    vel_coef = 1.0 + 0.5 * NOISE_SLOPE * NOISE_SLOPE
    w_in_full, w_down_full = gather_weights(w_in, w_down, ng, nd)
    latent_now = latents
    input_list = []
    hidden_list = []
    pre_list = []
    vgrad_list = []
    for step_num in range(2):
        sched_index = start_step + step_num
        time_now = 1.0 - sched_index.astype(jnp.float32) / SCHED
        onehot = (sched_index[:, None] == jnp.arange(SCHED, dtype=jnp.int32)[None, :]).astype(
            jnp.float32
        )
        mod_rows = jnp.einsum("is,scd->icd", onehot, modulation, precision=HIGH_PREC)
        normed = latent_now * lax.rsqrt(
            jnp.mean(latent_now * latent_now, axis=2, keepdims=True) + 1e-06
        )
        inputs = (normed * (1.0 + mod_rows[:, None, 1, :]) + mod_rows[:, None, 0, :]).astype(
            jnp.bfloat16
        )
        pre_act = jnp.einsum(
            "ild,df->ilf", inputs, w_in_full, preferred_element_type=jnp.float32
        ) / math.sqrt(model_width)
        activation, gelu_slope = gelu_parts(pre_act)
        hidden = activation.astype(jnp.bfloat16)
        partial_vel = jnp.einsum(
            "ilf,df->ild", hidden, w_down_full, preferred_element_type=jnp.float32
        ) / math.sqrt(hidden_width)
        velocity = sum_over_mp(partial_vel.astype(BF16), n, 2 + step_num).astype(jnp.float32)
        noise_level = (NOISE_SLOPE * jnp.sqrt(time_now / (1.0 - time_now)))[:, None, None]
        drift_x = (0.5 * NOISE_SLOPE * NOISE_SLOPE / (1.0 - time_now))[:, None, None]
        eps_draw = noise[:, step_num].astype(jnp.float32)
        ref_vel = ref_velocity[:, step_num].astype(jnp.float32)
        step_mean = latent_now * (1.0 - step_len * drift_x) - step_len * vel_coef * velocity
        latent_now = step_mean + noise_level * math.sqrt(step_len) * eps_draw
        policy_ratio = jnp.exp(behaviour_gap[:, step_num])
        active = (advantages >= 0.0) & (policy_ratio <= 1.0 + CLIP_RANGE) | (advantages < 0.0) & (
            policy_ratio >= 1.0 - CLIP_RANGE
        )
        pg_coef = jnp.where(active, policy_ratio * advantages, jnp.zeros_like(advantages))[
            :, None, None
        ]
        vel_grad = (
            pg_coef * vel_coef * math.sqrt(step_len) * eps_draw / noise_level
            + vel_coef * vel_coef * step_len * (velocity - ref_vel) / (noise_level * noise_level)
        ).astype(jnp.bfloat16)
        hid_grad = jnp.einsum(
            "ild,df->ilf", vel_grad, w_down_full, preferred_element_type=jnp.float32
        ) / math.sqrt(hidden_width)
        pre_list.append((hid_grad * gelu_slope).astype(jnp.bfloat16))
        input_list.append(inputs)
        hidden_list.append(hidden)
        vgrad_list.append(vel_grad)
    inputs_all = jnp.concatenate(input_list, axis=1)
    pre_all = jnp.concatenate(pre_list, axis=1)
    vgrad_all = jnp.concatenate(vgrad_list, axis=1)
    hidden_all = jnp.concatenate(hidden_list, axis=1)
    grad_in = jnp.einsum(
        "ild,ilf->df", inputs_all, pre_all, preferred_element_type=jnp.float32
    ) / math.sqrt(model_width)
    grad_down = jnp.einsum(
        "ild,ilf->df", vgrad_all, hidden_all, preferred_element_type=jnp.float32
    ) / math.sqrt(hidden_width)
    held = 6 * nd * w_in.size * 2 + 4 * w_in.size * 4
    update = update_weights if held < VMEM_LIMIT * 3 // 4 else update_by_ops
    new_in, new_down = update(grad_in.astype(BF16), grad_down.astype(BF16), w_in, w_down, ng, nd, n)
    return (latent_now, new_in, new_down)


def solution(mesh):
    return jax.shard_map(
        on_device,
        mesh=mesh,
        in_specs=(
            P(("group", "dp"), None, None),
            P(("group", "dp"), None, None, None),
            P(("group", "dp"), None, None, None),
            P(("group", "dp")),
            P(("group", "dp")),
            P(("group", "dp"), None),
            P(),
            P(("group", "dp"), "mp"),
            P(("group", "dp"), "mp"),
        ),
        out_specs=(
            P(("group", "dp"), None, None),
            P(("group", "dp"), "mp"),
            P(("group", "dp"), "mp"),
        ),
        check_vma=False,
    )
```

```python
import functools
import math

import jax
import jax.numpy as jnp
from jax import lax
from jax.experimental import pallas as pl
from jax.experimental.pallas import tpu as pltpu
from jax.sharding import PartitionSpec as P

SCHED = 10


NOISE_SLOPE = 0.7
CLIP_RANGE = 0.2
GELU_COEF = 0.7978845608028654
GELU_CUBE = 0.044715
HIGH_PREC = lax.Precision.HIGHEST
MESH = pl.DeviceIdType.MESH
F32 = jnp.float32
BF16 = jnp.bfloat16
VMEM_LIMIT = 56 * 1024 * 1024


def params(collective_id):
    return pltpu.CompilerParams(
        collective_id=collective_id, has_side_effects=True, vmem_limit_bytes=VMEM_LIMIT
    )


def remote(src, dst, send_sem, recv_sem, **axes):
    return pltpu.make_async_remote_copy(
        src_ref=src, dst_ref=dst, send_sem=send_sem, recv_sem=recv_sem,
        device_id=axes, device_id_type=MESH,
    )


def greet(peers):
    barrier = pltpu.get_barrier_semaphore()
    for axes in peers:
        pl.semaphore_signal(barrier, inc=1, device_id=axes, device_id_type=MESH)
    pl.semaphore_wait(barrier, len(peers))


def row_chunks(rows):
    parts = 2 if rows % 32 == 0 else 1
    size = rows // parts
    return [pl.ds(c * size, size) for c in range(parts)]


def sum_kernel(no, src, out, ybuf, zsum, zbuf, ys, yr, zs, zr, gzs, gzr, gys, gyr):
    m = lax.axis_index("mp")
    y, z = lax.rem(m, 2), lax.div(m, 2)
    partner = z * 2 + 1 - y
    ahead = [lax.rem(z + o, no) for o in range(no)]
    behind = [lax.rem(z - o + no, no) for o in range(no)]
    greet([{"mp": partner}] + [{"mp": ahead[o] * 2 + y} for o in range(1, no)])
    order = list(range(1, no)) + [0]
    pending = []
    for o in order:
        copy = remote(src.at[ahead[o] * 2 + 1 - y], ybuf.at[o], ys.at[o], yr.at[o], mp=partner)
        copy.start()
        pending.append(copy)
    for o in order[:-1]:
        remote(src.at[ahead[o] * 2 + 1 - y], ybuf.at[o], ys.at[o], yr.at[o], mp=partner).wait_recv()
        zsum[o] = (src[ahead[o] * 2 + y].astype(F32) + ybuf[o].astype(F32)).astype(BF16)
        copy = remote(zsum.at[o], zbuf.at[o], zs.at[o], zr.at[o], mp=ahead[o] * 2 + y)
        copy.start()
        pending.append(copy)
    remote(src.at[z * 2 + 1 - y], ybuf.at[0], ys.at[0], yr.at[0], mp=partner).wait_recv()
    total = src[m].astype(F32) + ybuf[0].astype(F32)
    for o in range(1, no):
        remote(zsum.at[o], zbuf.at[o], zs.at[o], zr.at[o], mp=ahead[o] * 2 + y).wait_recv()
        total = total + zbuf[o].astype(F32)
    out[m] = total.astype(BF16)
    for o in range(1, no):
        copy = remote(out.at[m], out.at[m], gzs.at[o], gzr.at[o], mp=ahead[o] * 2 + y)
        copy.start()
        pending.append(copy)
    copy = remote(out.at[m], out.at[m], gys.at[0], gyr.at[0], mp=partner)
    copy.start()
    pending.append(copy)
    for o in range(1, no):
        block = out.at[behind[o] * 2 + y]
        remote(block, block, gzs.at[o], gzr.at[o], mp=ahead[o] * 2 + y).wait_recv()
        copy = remote(block, block, gys.at[o], gyr.at[o], mp=partner)
        copy.start()
        pending.append(copy)
    for o in range(no):
        block = out.at[behind[o] * 2 + 1 - y]
        remote(block, block, gys.at[o], gyr.at[o], mp=partner).wait_recv()
    for copy in pending:
        copy.wait_send()


def sum_over_mp(part, n, collective_id):
    images, tokens, width = part.shape
    no, rows = n // 2, images * tokens // n
    dma = pltpu.SemaphoreType.DMA
    vmem = pl.BlockSpec(memory_space=pltpu.VMEM)
    summed = pl.pallas_call(
        functools.partial(sum_kernel, no),
        out_shape=jax.ShapeDtypeStruct((n, rows, width), BF16),
        in_specs=[vmem],
        out_specs=vmem,
        scratch_shapes=[pltpu.VMEM((no, rows, width), BF16)] * 3 + [dma((no,))] * 8,
        compiler_params=params(collective_id),
        name="sum_over_mp",
    )(part.reshape(n, rows, width))
    return summed.reshape(images, tokens, width)


def update_kernel(
    nd, n, count, scales, lhs_down, rhs_down, lhs_in, rhs_in, w_down, w_in, new_down, new_in,
    out_buf, sib, far, total, sq_mp, sq_gd, cs, cr, xs, xr, ms, mr, ps, pr,
):
    g, d, m = lax.axis_index("group"), lax.axis_index("dp"), lax.axis_index("mp")
    other = 1 - g
    targets = [lax.rem(d + o, nd) for o in range(nd)]
    mp_peers = [lax.rem(m + o, n) for o in range(n)]
    gd_peers = [(h, o) for h in range(2) for o in range(nd)]
    place = lambda h: g if h == 0 else other
    greet(
        [{"group": place(h), "dp": targets[o]} for h, o in gd_peers[1:]]
        + [{"mp": mp_peers[o]} for o in range(1, n)]
    )
    rows = w_in.shape[0]
    chunks = row_chunks(rows)
    order = list(range(1, nd)) + [0]
    sides = ((lhs_down, rhs_down), (lhs_in, rhs_in))
    pending = []
    far_sends = {}
    step = 16 if chunks[0].size % 16 == 0 else chunks[0].size

    def tiles(part, body, init):
        return lax.fori_loop(
            0, part.size // step,
            lambda i, v: body(pl.ds(pl.multiple_of(part.start + i * step, step), step), v), init,
        )

    def block(a, index, part):
        lhs, rhs = sides[a]
        return jnp.dot(lhs[index, part], rhs[...], preferred_element_type=F32) * scales[a]

    for o in order:
        for a in range(2):
            copies = []
            for c, part in enumerate(chunks):
                out_buf[a, o, part] = block(a, other * nd + targets[o], part).astype(BF16)
                copy = remote(
                    out_buf.at[a, o, part], sib.at[a, o, part], cs.at[a, o, c], cr.at[a, o, c], group=other
                )
                copy.start()
                copies.append(copy)
            for c, part in enumerate(chunks):
                total[a, part] = block(a, g * nd + targets[o], part)
                copies[c].wait_recv()

                def add(at, _):
                    value = total[a, at] + sib[a, o, at].astype(F32)
                    if o:
                        sib[a, o, at] = value.astype(BF16)
                    else:
                        total[a, at] = value
                    return 0

                tiles(part, add, 0)
                if o:
                    send = remote(
                        sib.at[a, o, part], far.at[a, o - 1, part], xs.at[a, o, c], xr.at[a, o, c], dp=targets[o]
                    )
                    send.start()
                    pending.append(send)
                    far_sends[a, o, c] = send
            pending += copies
    square = jnp.zeros((step, w_in.shape[1]), F32)
    for a in range(2):
        for c, part in enumerate(chunks):
            for o in order[:-1]:
                far_sends[a, o, c].wait_recv()

            def finish(at, sq):
                value = total[a, at]
                for o in order[:-1]:
                    value = value + far[a, o - 1, at].astype(F32)
                total[a, at] = value
                return sq + value * value

            square = tiles(part, finish, square)
    sq_mp[0] = jnp.full((8, 128), jnp.sum(square), F32)
    sends = []
    for o in range(1, n):
        copy = remote(sq_mp.at[0], sq_mp.at[o], ms.at[o], mr.at[o], mp=mp_peers[o])
        copy.start()
        sends.append(copy)
    for copy in sends:
        copy.wait_recv()
    pending += sends
    value = sq_mp[0]
    for o in range(1, n):
        value = value + sq_mp[o]
    sq_gd[0] = value
    sends = []
    for p, (h, o) in enumerate(gd_peers):
        if p:
            copy = remote(sq_gd.at[0], sq_gd.at[p], ps.at[p], pr.at[p], group=place(h), dp=targets[o])
            copy.start()
            sends.append(copy)
    for copy in sends:
        copy.wait_recv()
    pending += sends
    for p in range(1, len(gd_peers)):
        value = value + sq_gd[p]
    inverse = lax.rsqrt(value[0:1, 0:1] / count + 1e-06)
    for a, (w, new) in enumerate(((w_down, new_down), (w_in, new_in))):

        def update(at, _):
            new[at] = (w[at].astype(F32) - total[a, at] * inverse).astype(BF16)
            return 0

        tiles(pl.ds(0, rows), update, 0)
    for copy in pending:
        copy.wait_send()


def update_weights(inputs, pre, vgrad, hidden, w_in, w_down, ng, nd, n, scales):
    rows, units = w_in.shape
    nc = len(row_chunks(rows))
    count = 2.0 * rows * ng * nd * units * n
    dma = pltpu.SemaphoreType.DMA
    vmem = pl.BlockSpec(memory_space=pltpu.VMEM)
    shape = jax.ShapeDtypeStruct((rows, units), w_in.dtype)
    turned = lambda x: x.reshape(-1, x.shape[-1]).T.reshape(ng * nd, rows, -1)
    new_down, new_in = pl.pallas_call(
        functools.partial(update_kernel, nd, n, count, scales),
        out_shape=(shape, shape),
        in_specs=[vmem] * 6,
        out_specs=(vmem, vmem),
        scratch_shapes=[
            pltpu.VMEM((2, nd, rows, units), BF16),
            pltpu.VMEM((2, nd, rows, units), BF16),
            pltpu.VMEM((2, nd - 1, rows, units), BF16),
            pltpu.VMEM((2, rows, units), F32),
            pltpu.VMEM((n, 8, 128), F32),
            pltpu.VMEM((ng * nd, 8, 128), F32),
            dma((2, nd, nc)), dma((2, nd, nc)), dma((2, nd, nc)), dma((2, nd, nc)),
            dma((n,)), dma((n,)), dma((ng * nd,)), dma((ng * nd,)),
        ],
        compiler_params=params(4),
        name="update_weights",
    )(
        turned(vgrad), hidden.reshape(-1, units), turned(inputs), pre.reshape(-1, units), w_down, w_in
    )
    return new_in, new_down


def update_by_ops(inputs, pre, vgrad, hidden, w_in, w_down, ng, nd, n, scales):
    rows, units = w_in.shape
    count = 2.0 * rows * ng * nd * units * n
    grads = (
        jnp.einsum("ild,ilf->df", inputs, pre, preferred_element_type=F32) * scales[1],
        jnp.einsum("ild,ilf->df", vgrad, hidden, preferred_element_type=F32) * scales[0],
    )
    mine = [
        lax.psum_scatter(grad.astype(BF16), ("group", "dp"), scatter_dimension=0, tiled=True).astype(F32)
        for grad in grads
    ]
    total = lax.psum(sum(jnp.sum(grad * grad) for grad in mine), ("group", "dp", "mp"))
    rms = jnp.sqrt(total / count + 1e-06)
    return tuple(
        (w.astype(F32) - grad / rms).astype(BF16) for w, grad in zip((w_in, w_down), mine)
    )


def gelu_parts(pre_act):
    tangent = jnp.tanh(GELU_COEF * (pre_act + GELU_CUBE * pre_act * pre_act * pre_act))
    activation = 0.5 * pre_act * (1.0 + tangent)
    gelu_slope = 0.5 * (1.0 + tangent) + 0.5 * pre_act * (1.0 - tangent * tangent) * GELU_COEF * (
        1.0 + 3.0 * GELU_CUBE * pre_act * pre_act
    )
    return (activation, gelu_slope)


def on_device(
    latents, noise, ref_velocity, start_step, advantages, behaviour_gap, modulation, w_in, w_down
):
    model_width = latents.shape[2]
    shard_units = w_in.shape[1]
    ng, nd, n = lax.axis_size("group"), lax.axis_size("dp"), lax.axis_size("mp")
    hidden_width = shard_units * n
    step_len = 1.0 / SCHED
    vel_coef = 1.0 + 0.5 * NOISE_SLOPE * NOISE_SLOPE
    w_in_full, w_down_full = (
        lax.all_gather(w_in, ("group", "dp"), axis=0, tiled=True),
        lax.all_gather(w_down, ("group", "dp"), axis=0, tiled=True),
    )
    latent_now = latents
    input_list = []
    hidden_list = []
    pre_list = []
    vgrad_list = []
    for step_num in range(2):
        sched_index = start_step + step_num
        time_now = 1.0 - sched_index.astype(jnp.float32) / SCHED
        onehot = (sched_index[:, None] == jnp.arange(SCHED, dtype=jnp.int32)[None, :]).astype(
            jnp.float32
        )
        mod_rows = jnp.einsum("is,scd->icd", onehot, modulation, precision=HIGH_PREC)
        normed = latent_now * lax.rsqrt(
            jnp.mean(latent_now * latent_now, axis=2, keepdims=True) + 1e-06
        )
        inputs = (normed * (1.0 + mod_rows[:, None, 1, :]) + mod_rows[:, None, 0, :]).astype(
            jnp.bfloat16
        )
        pre_act = jnp.einsum(
            "ild,df->ilf", inputs, w_in_full, preferred_element_type=jnp.float32
        ) / math.sqrt(model_width)
        activation, gelu_slope = gelu_parts(pre_act)
        hidden = activation.astype(jnp.bfloat16)
        partial_vel = jnp.einsum(
            "ilf,df->ild", hidden, w_down_full, preferred_element_type=jnp.float32
        ) / math.sqrt(hidden_width)
        velocity = sum_over_mp(partial_vel.astype(BF16), n, 2 + step_num).astype(jnp.float32)
        noise_level = (NOISE_SLOPE * jnp.sqrt(time_now / (1.0 - time_now)))[:, None, None]
        drift_x = (0.5 * NOISE_SLOPE * NOISE_SLOPE / (1.0 - time_now))[:, None, None]
        eps_draw = noise[:, step_num].astype(jnp.float32)
        ref_vel = ref_velocity[:, step_num].astype(jnp.float32)
        step_mean = latent_now * (1.0 - step_len * drift_x) - step_len * vel_coef * velocity
        latent_now = step_mean + noise_level * math.sqrt(step_len) * eps_draw
        policy_ratio = jnp.exp(behaviour_gap[:, step_num])
        active = (advantages >= 0.0) & (policy_ratio <= 1.0 + CLIP_RANGE) | (advantages < 0.0) & (
            policy_ratio >= 1.0 - CLIP_RANGE
        )
        pg_coef = jnp.where(active, policy_ratio * advantages, jnp.zeros_like(advantages))[
            :, None, None
        ]
        vel_grad = (
            pg_coef * vel_coef * math.sqrt(step_len) * eps_draw / noise_level
            + vel_coef * vel_coef * step_len * (velocity - ref_vel) / (noise_level * noise_level)
        ).astype(jnp.bfloat16)
        hid_grad = jnp.einsum(
            "ild,df->ilf", vel_grad, w_down_full, preferred_element_type=jnp.float32
        ) / math.sqrt(hidden_width)
        pre_list.append((hid_grad * gelu_slope).astype(jnp.bfloat16))
        input_list.append(inputs)
        hidden_list.append(hidden)
        vgrad_list.append(vel_grad)
    inputs_all = jnp.concatenate(input_list, axis=1)
    pre_all = jnp.concatenate(pre_list, axis=1)
    vgrad_all = jnp.concatenate(vgrad_list, axis=1)
    hidden_all = jnp.concatenate(hidden_list, axis=1)
    held = (6 * nd + 6) * w_in.size * 2 + 2 * (inputs_all.size + pre_all.size) * 2
    update = update_weights if held < VMEM_LIMIT * 7 // 8 else update_by_ops
    scales = (1.0 / math.sqrt(hidden_width), 1.0 / math.sqrt(model_width))
    new_in, new_down = update(
        inputs_all, pre_all, vgrad_all, hidden_all, w_in, w_down, ng, nd, n, scales
    )
    return (latent_now, new_in, new_down)


def solution(mesh):
    return jax.shard_map(
        on_device,
        mesh=mesh,
        in_specs=(
            P(("group", "dp"), None, None),
            P(("group", "dp"), None, None, None),
            P(("group", "dp"), None, None, None),
            P(("group", "dp")),
            P(("group", "dp")),
            P(("group", "dp"), None),
            P(),
            P(("group", "dp"), "mp"),
            P(("group", "dp"), "mp"),
        ),
        out_specs=(
            P(("group", "dp"), None, None),
            P(("group", "dp"), "mp"),
            P(("group", "dp"), "mp"),
        ),
        check_vma=False,
    )
```

```python
import functools
import math

import jax
import jax.numpy as jnp
from jax import lax
from jax.experimental import pallas as pl
from jax.experimental.pallas import tpu as pltpu
from jax.sharding import PartitionSpec as P

SCHED = 10


NOISE_SLOPE = 0.7
CLIP_RANGE = 0.2
GELU_COEF = 0.7978845608028654
GELU_CUBE = 0.044715
HIGH_PREC = lax.Precision.HIGHEST
MESH = pl.DeviceIdType.MESH
F32 = jnp.float32
BF16 = jnp.bfloat16
VMEM_LIMIT = 56 * 1024 * 1024


def params(collective_id):
    return pltpu.CompilerParams(
        collective_id=collective_id, has_side_effects=True, vmem_limit_bytes=VMEM_LIMIT
    )


def remote(src, dst, send_sem, recv_sem, **axes):
    return pltpu.make_async_remote_copy(
        src_ref=src, dst_ref=dst, send_sem=send_sem, recv_sem=recv_sem,
        device_id=axes, device_id_type=MESH,
    )


def greet(peers):
    barrier = pltpu.get_barrier_semaphore()
    for axes in peers:
        pl.semaphore_signal(barrier, inc=1, device_id=axes, device_id_type=MESH)
    pl.semaphore_wait(barrier, len(peers))


def row_chunks(rows):
    parts = 2 if rows % 32 == 0 else 1
    size = rows // parts
    return [pl.ds(c * size, size) for c in range(parts)]


def sum_kernel(no, src, out, ybuf, zsum, zbuf, ys, yr, zs, zr, gzs, gzr, gys, gyr):
    m = lax.axis_index("mp")
    y, z = lax.rem(m, 2), lax.div(m, 2)
    partner = z * 2 + 1 - y
    ahead = [lax.rem(z + o, no) for o in range(no)]
    behind = [lax.rem(z - o + no, no) for o in range(no)]
    greet([{"mp": partner}] + [{"mp": ahead[o] * 2 + y} for o in range(1, no)])
    order = list(range(1, no)) + [0]
    pending = []
    for o in order:
        copy = remote(src.at[ahead[o] * 2 + 1 - y], ybuf.at[o], ys.at[o], yr.at[o], mp=partner)
        copy.start()
        pending.append(copy)
    for o in order[:-1]:
        remote(src.at[ahead[o] * 2 + 1 - y], ybuf.at[o], ys.at[o], yr.at[o], mp=partner).wait_recv()
        zsum[o] = (src[ahead[o] * 2 + y].astype(F32) + ybuf[o].astype(F32)).astype(BF16)
        copy = remote(zsum.at[o], zbuf.at[o], zs.at[o], zr.at[o], mp=ahead[o] * 2 + y)
        copy.start()
        pending.append(copy)
    remote(src.at[z * 2 + 1 - y], ybuf.at[0], ys.at[0], yr.at[0], mp=partner).wait_recv()
    total = src[m].astype(F32) + ybuf[0].astype(F32)
    for o in range(1, no):
        remote(zsum.at[o], zbuf.at[o], zs.at[o], zr.at[o], mp=ahead[o] * 2 + y).wait_recv()
        total = total + zbuf[o].astype(F32)
    out[m] = total.astype(BF16)
    for o in range(1, no):
        copy = remote(out.at[m], out.at[m], gzs.at[o], gzr.at[o], mp=ahead[o] * 2 + y)
        copy.start()
        pending.append(copy)
    copy = remote(out.at[m], out.at[m], gys.at[0], gyr.at[0], mp=partner)
    copy.start()
    pending.append(copy)
    for o in range(1, no):
        block = out.at[behind[o] * 2 + y]
        remote(block, block, gzs.at[o], gzr.at[o], mp=ahead[o] * 2 + y).wait_recv()
        copy = remote(block, block, gys.at[o], gyr.at[o], mp=partner)
        copy.start()
        pending.append(copy)
    for o in range(no):
        block = out.at[behind[o] * 2 + 1 - y]
        remote(block, block, gys.at[o], gyr.at[o], mp=partner).wait_recv()
    for copy in pending:
        copy.wait_send()


def sum_over_mp(part, n, collective_id):
    images, tokens, width = part.shape
    no, rows = n // 2, images * tokens // n
    dma = pltpu.SemaphoreType.DMA
    vmem = pl.BlockSpec(memory_space=pltpu.VMEM)
    summed = pl.pallas_call(
        functools.partial(sum_kernel, no),
        out_shape=jax.ShapeDtypeStruct((n, rows, width), BF16),
        in_specs=[vmem],
        out_specs=vmem,
        scratch_shapes=[pltpu.VMEM((no, rows, width), BF16)] * 3 + [dma((no,))] * 8,
        compiler_params=params(collective_id),
        name="sum_over_mp",
    )(part.reshape(n, rows, width))
    return summed.reshape(images, tokens, width)


def update_kernel(
    nd, n, count, scales, lhs_down, rhs_down, lhs_in, rhs_in, w_down, w_in, new_down, new_in,
    turned, out_buf, sib, far, total, sq_mp, sq_gd, cs, cr, xs, xr, ms, mr, ps, pr,
):
    g, d, m = lax.axis_index("group"), lax.axis_index("dp"), lax.axis_index("mp")
    other = 1 - g
    targets = [lax.rem(d + o, nd) for o in range(nd)]
    mp_peers = [lax.rem(m + o, n) for o in range(n)]
    gd_peers = [(h, o) for h in range(2) for o in range(nd)]
    place = lambda h: g if h == 0 else other
    greet(
        [{"group": place(h), "dp": targets[o]} for h, o in gd_peers[1:]]
        + [{"mp": mp_peers[o]} for o in range(1, n)]
    )
    rows = w_in.shape[0]
    chunks = row_chunks(rows)
    order = list(range(1, nd)) + [0]
    sides = ((lhs_down, rhs_down), (lhs_in, rhs_in))
    pending = []
    far_sends = {}
    step = 16 if chunks[0].size % 16 == 0 else chunks[0].size

    def tiles(part, body, init):
        return lax.fori_loop(
            0, part.size // step,
            lambda i, v: body(pl.ds(pl.multiple_of(part.start + i * step, step), step), v), init,
        )

    def block(a, index, part):
        at = pl.ds(pl.multiple_of(index * rows + part.start, 8), part.size)
        return jnp.dot(turned[a, at], sides[a][1][...], preferred_element_type=F32) * scales[a]

    def turn(a):
        lhs = sides[a][0]

        def body(t, _):
            at = pl.ds(pl.multiple_of(t * 128, 128), 128)
            turned[a, at] = lhs[:, at].T
            return 0

        lax.fori_loop(0, lhs.shape[1] // 128, body, 0)

    for o in order:
        for a in range(2):
            copies = []
            if o == order[0]:
                turn(a)
            for c, part in enumerate(chunks):
                out_buf[a, o, part] = block(a, other * nd + targets[o], part).astype(BF16)
                copy = remote(
                    out_buf.at[a, o, part], sib.at[a, o, part], cs.at[a, o, c], cr.at[a, o, c], group=other
                )
                copy.start()
                copies.append(copy)
            for c, part in enumerate(chunks):
                total[a, part] = block(a, g * nd + targets[o], part)
                copies[c].wait_recv()

                def add(at, _):
                    value = total[a, at] + sib[a, o, at].astype(F32)
                    if o:
                        sib[a, o, at] = value.astype(BF16)
                    else:
                        total[a, at] = value
                    return 0

                tiles(part, add, 0)
                if o:
                    send = remote(
                        sib.at[a, o, part], far.at[a, o - 1, part], xs.at[a, o, c], xr.at[a, o, c], dp=targets[o]
                    )
                    send.start()
                    pending.append(send)
                    far_sends[a, o, c] = send
            pending += copies
    square = jnp.zeros((step, w_in.shape[1]), F32)
    for a in range(2):
        for c, part in enumerate(chunks):
            for o in order[:-1]:
                far_sends[a, o, c].wait_recv()

            def finish(at, sq):
                value = total[a, at]
                for o in order[:-1]:
                    value = value + far[a, o - 1, at].astype(F32)
                total[a, at] = value
                return sq + value * value

            square = tiles(part, finish, square)
    sq_mp[0] = jnp.full((8, 128), jnp.sum(square), F32)
    sends = []
    for o in range(1, n):
        copy = remote(sq_mp.at[0], sq_mp.at[o], ms.at[o], mr.at[o], mp=mp_peers[o])
        copy.start()
        sends.append(copy)
    for copy in sends:
        copy.wait_recv()
    pending += sends
    value = sq_mp[0]
    for o in range(1, n):
        value = value + sq_mp[o]
    sq_gd[0] = value
    sends = []
    for p, (h, o) in enumerate(gd_peers):
        if p:
            copy = remote(sq_gd.at[0], sq_gd.at[p], ps.at[p], pr.at[p], group=place(h), dp=targets[o])
            copy.start()
            sends.append(copy)
    for copy in sends:
        copy.wait_recv()
    pending += sends
    for p in range(1, len(gd_peers)):
        value = value + sq_gd[p]
    inverse = lax.rsqrt(value[0:1, 0:1] / count + 1e-06)
    for a, (w, new) in enumerate(((w_down, new_down), (w_in, new_in))):

        def update(at, _):
            new[at] = (w[at].astype(F32) - total[a, at] * inverse).astype(BF16)
            return 0

        tiles(pl.ds(0, rows), update, 0)
    for copy in pending:
        copy.wait_send()


def update_weights(inputs, pre, vgrad, hidden, w_in, w_down, ng, nd, n, scales):
    rows, units = w_in.shape
    nc = len(row_chunks(rows))
    count = 2.0 * rows * ng * nd * units * n
    dma = pltpu.SemaphoreType.DMA
    vmem = pl.BlockSpec(memory_space=pltpu.VMEM)
    shape = jax.ShapeDtypeStruct((rows, units), w_in.dtype)
    flat = lambda x: x.reshape(-1, x.shape[-1])
    tokens = flat(inputs).shape[0]
    new_down, new_in = pl.pallas_call(
        functools.partial(update_kernel, nd, n, count, scales),
        out_shape=(shape, shape),
        in_specs=[vmem] * 6,
        out_specs=(vmem, vmem),
        scratch_shapes=[
            pltpu.VMEM((2, ng * nd * rows, tokens), BF16),
            pltpu.VMEM((2, nd, rows, units), BF16),
            pltpu.VMEM((2, nd, rows, units), BF16),
            pltpu.VMEM((2, nd - 1, rows, units), BF16),
            pltpu.VMEM((2, rows, units), F32),
            pltpu.VMEM((n, 8, 128), F32),
            pltpu.VMEM((ng * nd, 8, 128), F32),
            dma((2, nd, nc)), dma((2, nd, nc)), dma((2, nd, nc)), dma((2, nd, nc)),
            dma((n,)), dma((n,)), dma((ng * nd,)), dma((ng * nd,)),
        ],
        compiler_params=params(4),
        name="update_weights",
    )(
        flat(vgrad), flat(hidden), flat(inputs), flat(pre), w_down, w_in
    )
    return new_in, new_down


def update_by_ops(inputs, pre, vgrad, hidden, w_in, w_down, ng, nd, n, scales):
    rows, units = w_in.shape
    count = 2.0 * rows * ng * nd * units * n
    grads = (
        jnp.einsum("ild,ilf->df", inputs, pre, preferred_element_type=F32) * scales[1],
        jnp.einsum("ild,ilf->df", vgrad, hidden, preferred_element_type=F32) * scales[0],
    )
    mine = [
        lax.psum_scatter(grad.astype(BF16), ("group", "dp"), scatter_dimension=0, tiled=True).astype(F32)
        for grad in grads
    ]
    total = lax.psum(sum(jnp.sum(grad * grad) for grad in mine), ("group", "dp", "mp"))
    rms = jnp.sqrt(total / count + 1e-06)
    return tuple(
        (w.astype(F32) - grad / rms).astype(BF16) for w, grad in zip((w_in, w_down), mine)
    )


def gelu_parts(pre_act):
    tangent = jnp.tanh(GELU_COEF * (pre_act + GELU_CUBE * pre_act * pre_act * pre_act))
    activation = 0.5 * pre_act * (1.0 + tangent)
    gelu_slope = 0.5 * (1.0 + tangent) + 0.5 * pre_act * (1.0 - tangent * tangent) * GELU_COEF * (
        1.0 + 3.0 * GELU_CUBE * pre_act * pre_act
    )
    return (activation, gelu_slope)


def on_device(
    latents, noise, ref_velocity, start_step, advantages, behaviour_gap, modulation, w_in, w_down
):
    model_width = latents.shape[2]
    shard_units = w_in.shape[1]
    ng, nd, n = lax.axis_size("group"), lax.axis_size("dp"), lax.axis_size("mp")
    hidden_width = shard_units * n
    step_len = 1.0 / SCHED
    vel_coef = 1.0 + 0.5 * NOISE_SLOPE * NOISE_SLOPE
    w_in_full, w_down_full = (
        lax.all_gather(w_in, ("group", "dp"), axis=0, tiled=True),
        lax.all_gather(w_down, ("group", "dp"), axis=0, tiled=True),
    )
    latent_now = latents
    input_list = []
    hidden_list = []
    pre_list = []
    vgrad_list = []
    for step_num in range(2):
        sched_index = start_step + step_num
        time_now = 1.0 - sched_index.astype(jnp.float32) / SCHED
        onehot = (sched_index[:, None] == jnp.arange(SCHED, dtype=jnp.int32)[None, :]).astype(
            jnp.float32
        )
        mod_rows = jnp.einsum("is,scd->icd", onehot, modulation, precision=HIGH_PREC)
        normed = latent_now * lax.rsqrt(
            jnp.mean(latent_now * latent_now, axis=2, keepdims=True) + 1e-06
        )
        inputs = (normed * (1.0 + mod_rows[:, None, 1, :]) + mod_rows[:, None, 0, :]).astype(
            jnp.bfloat16
        )
        pre_act = jnp.einsum(
            "ild,df->ilf", inputs, w_in_full, preferred_element_type=jnp.float32
        ) / math.sqrt(model_width)
        activation, gelu_slope = gelu_parts(pre_act)
        hidden = activation.astype(jnp.bfloat16)
        partial_vel = jnp.einsum(
            "ilf,df->ild", hidden, w_down_full, preferred_element_type=jnp.float32
        ) / math.sqrt(hidden_width)
        velocity = sum_over_mp(partial_vel.astype(BF16), n, 2 + step_num).astype(jnp.float32)
        noise_level = (NOISE_SLOPE * jnp.sqrt(time_now / (1.0 - time_now)))[:, None, None]
        drift_x = (0.5 * NOISE_SLOPE * NOISE_SLOPE / (1.0 - time_now))[:, None, None]
        eps_draw = noise[:, step_num].astype(jnp.float32)
        ref_vel = ref_velocity[:, step_num].astype(jnp.float32)
        step_mean = latent_now * (1.0 - step_len * drift_x) - step_len * vel_coef * velocity
        latent_now = step_mean + noise_level * math.sqrt(step_len) * eps_draw
        policy_ratio = jnp.exp(behaviour_gap[:, step_num])
        active = (advantages >= 0.0) & (policy_ratio <= 1.0 + CLIP_RANGE) | (advantages < 0.0) & (
            policy_ratio >= 1.0 - CLIP_RANGE
        )
        pg_coef = jnp.where(active, policy_ratio * advantages, jnp.zeros_like(advantages))[
            :, None, None
        ]
        vel_grad = (
            pg_coef * vel_coef * math.sqrt(step_len) * eps_draw / noise_level
            + vel_coef * vel_coef * step_len * (velocity - ref_vel) / (noise_level * noise_level)
        ).astype(jnp.bfloat16)
        hid_grad = jnp.einsum(
            "ild,df->ilf", vel_grad, w_down_full, preferred_element_type=jnp.float32
        ) / math.sqrt(hidden_width)
        pre_list.append((hid_grad * gelu_slope).astype(jnp.bfloat16))
        input_list.append(inputs)
        hidden_list.append(hidden)
        vgrad_list.append(vel_grad)
    inputs_all = jnp.concatenate(input_list, axis=1)
    pre_all = jnp.concatenate(pre_list, axis=1)
    vgrad_all = jnp.concatenate(vgrad_list, axis=1)
    hidden_all = jnp.concatenate(hidden_list, axis=1)
    held = (6 * nd + 6) * w_in.size * 2 + 2 * (2 * inputs_all.size + pre_all.size) * 2
    update = update_weights if held < VMEM_LIMIT * 7 // 8 else update_by_ops
    scales = (1.0 / math.sqrt(hidden_width), 1.0 / math.sqrt(model_width))
    new_in, new_down = update(
        inputs_all, pre_all, vgrad_all, hidden_all, w_in, w_down, ng, nd, n, scales
    )
    return (latent_now, new_in, new_down)


def solution(mesh):
    return jax.shard_map(
        on_device,
        mesh=mesh,
        in_specs=(
            P(("group", "dp"), None, None),
            P(("group", "dp"), None, None, None),
            P(("group", "dp"), None, None, None),
            P(("group", "dp")),
            P(("group", "dp")),
            P(("group", "dp"), None),
            P(),
            P(("group", "dp"), "mp"),
            P(("group", "dp"), "mp"),
        ),
        out_specs=(
            P(("group", "dp"), None, None),
            P(("group", "dp"), "mp"),
            P(("group", "dp"), "mp"),
        ),
        check_vma=False,
    )
```
